32 devices in a mesh: dp: 4 (over z), table: 8 (over y, x, core).
Axes of the slice: x: 2, y: 2, z: 4, core: 2. Of those that a mesh axis runs over, the one named last changes fastest.
Arguments:
- dense_feats: bfloat16 [4096, 13], P(('dp', 'table')), may hold values from -6 to 6
- lookup_ids: int32 [32, 8, 4096], P('table', None, 'dp'), may hold values from 0 to 2047
- lookup_counts: int32 [32, 4096], P('table', 'dp'), may hold values from 0 to 8
- shard_table: int32 [32], replicated, may hold values from 0 to 25, as said below
- embed_tables: bfloat16 [32, 2048, 128], P('table'), may hold values from -6 to 6
- first_layer: bfloat16 [13, 512], replicated, may hold values from -1.75 to 1.75
- first_offset: float32 [512], replicated, may hold values from -3 to 3
- second_layer: bfloat16 [512, 256], replicated, may hold values from -0.25 to 0.25
- second_offset: float32 [256], replicated, may hold values from -3 to 3
- third_layer: bfloat16 [256, 128], replicated, may hold values from -0.375 to 0.375
- third_offset: float32 [128], replicated, may hold values from -3 to 3
- cross_down: bfloat16 [3456, 512], P(None, 'table'), may hold values from -0.109375 to 0.109375
- cross_up: bfloat16 [512, 3456], P('table'), may hold values from -0.25 to 0.25
- cross_bias: float32 [3456], replicated, may hold values from -3 to 3
- cotangent: bfloat16 [4096, 3456], P(('dp', 'table')), may hold values from -0.059814453 to 0.059814453
Outputs:
- table_grad: float32 [32, 2048, 128], P('table', 'dp')
- first_layer_grad: float32 [13, 512], replicated
- first_offset_grad: float32 [512], replicated
- second_layer_grad: float32 [512, 256], replicated
- second_offset_grad: float32 [256], replicated
- third_layer_grad: float32 [256, 128], replicated
- third_offset_grad: float32 [128], replicated
- cross_bias_grad: float32 [3456], replicated
The draws below stay inside these ranges and needn't reach their ends.
Inputs may be any that keep to these rules, and one draw needn't show every extreme that they name: `shard_table`: every table has at least one shard.
All inputs are finite; a program needn't handle non-finite values.
Results may differ from the reference program's by a relative error of at most 0.0085.
Values may be sent and summed in bfloat16 or wider, within the bound.
A program may use at most 64 MiB of HBM per device.

```python
import math
import jax
import jax.numpy as jnp
import numpy as np
from jax import lax

TABLES = 26
EMB = 128
DENSE = 13
H1 = 512
H2 = 256
RANK = 512
SHARDS = 32
HOT = 8
ROWS = 2048
EX_DEV = 128
CROSS_IN = 3456
BATCH = 4096
N_DP = 4
N_TABLE = 8


def draw_shard_table(key, part):
    first_key, second_key = jax.random.split(jax.random.fold_in(key, 17))
    extra = jax.random.randint(first_key, (SHARDS - TABLES,), 0, TABLES).astype(jnp.int32)
    base = jnp.concatenate([jnp.arange(TABLES, dtype=jnp.int32), extra])
    order = jax.random.permutation(second_key, SHARDS)
    return base[order]


def touch_ends(drawn, key, smallest, largest):
    place = [jax.random.randint(jax.random.fold_in(key, axis), (), 0, length) for axis, length in enumerate(drawn.shape)]
    widest = drawn.shape.index(max(drawn.shape))
    neighbour = place[:widest] + [(place[widest] + 1) % drawn.shape[widest]] + place[widest + 1:]
    return drawn.at[tuple(place)].set(smallest).at[tuple(neighbour)].set(largest)


def block_scale(rng, dims, shards, low, high):
    level = 1.0
    for position, blocks in shards:
        steps = jax.random.uniform(jax.random.fold_in(jax.random.fold_in(rng, 6), position), (blocks,), jnp.float32, low / len(shards), high / len(shards))
        level = level * jnp.repeat(jnp.exp(steps), dims[position] // blocks).reshape((-1,) + (1,) * (len(dims) - 1 - position))
    return level


def rank_table(number_of, slope):
    loads = [(1 << 20) // math.isqrt(rank ** slope) + 1 for rank in range(1, number_of + 1)]
    scale = 1 + sum(loads) // (1 << 30)
    return np.cumsum(np.array([max(1, weight // scale) for weight in loads]))


def skewed_ids(rng, shape, number_of, slope):
    listing = rank_table(number_of, slope)
    lot = jax.random.randint(jax.random.fold_in(rng, 1), shape, 0, int(listing[number_of - 1]))
    standing = jnp.searchsorted(jnp.asarray(listing, jnp.int32), lot, side="right")
    return jax.random.permutation(jax.random.fold_in(rng, 2), number_of)[standing].astype(jnp.int32)


def normal_values(stream_key, shape, deviation, most, cuts=(), kind=jnp.bfloat16):
    values = jax.random.normal(stream_key, shape, jnp.float32) * deviation
    if len(cuts) > 0:
        values = block_scale(stream_key, shape, cuts, -0.22, 0.18) * values
    return jnp.clip(values, min=-most, max=most).astype(kind)


def setup_inputs(seed: int = 0) -> dict:
    splits = jax.random.split(jax.random.key(seed), 16)
    dense_feats = normal_values(splits[0], (BATCH, DENSE), 1.0, 6.0, ((0, 32),))
    lookup_ids = touch_ends(skewed_ids(splits[1], (SHARDS, HOT, BATCH), ROWS, 2), jax.random.fold_in(splits[1], 3), 0, ROWS - 1).astype(jnp.int32)
    lookup_counts = touch_ends(jax.random.randint(splits[2], (SHARDS, BATCH), 0, HOT + 1), jax.random.fold_in(splits[2], 1), 0, HOT).astype(jnp.int32)
    shard_table = draw_shard_table(jax.random.fold_in(splits[15], 71), 0)
    embed_tables = normal_values(splits[4], (SHARDS, ROWS, EMB), 1.0, 6.0, ((0, 8),))
    first_layer = normal_values(splits[5], (DENSE, H1), DENSE ** -0.5, 1.75)
    first_offset = normal_values(splits[6], (H1,), 0.5, 3.0, (), jnp.float32)
    second_layer = normal_values(splits[7], (H1, H2), H1 ** -0.5, 0.25)
    second_offset = normal_values(splits[8], (H2,), 0.5, 3.0, (), jnp.float32)
    third_layer = normal_values(splits[9], (H2, EMB), H2 ** -0.5, 0.375)
    third_offset = normal_values(splits[10], (EMB,), 0.5, 3.0, (), jnp.float32)
    cross_down = normal_values(splits[11], (CROSS_IN, RANK), CROSS_IN ** -0.5, 0.109375, ((1, 8),))
    cross_up = normal_values(splits[12], (RANK, CROSS_IN), RANK ** -0.5, 0.25, ((0, 8),))
    cross_bias = normal_values(splits[13], (CROSS_IN,), 0.5, 3.0, (), jnp.float32)
    cotangent = normal_values(splits[14], (BATCH, CROSS_IN), 0.01, 0.059814453, ((0, 32),))
    return {"dense_feats": dense_feats, "lookup_ids": lookup_ids, "lookup_counts": lookup_counts, "shard_table": shard_table, "embed_tables": embed_tables, "first_layer": first_layer, "first_offset": first_offset, "second_layer": second_layer, "second_offset": second_offset, "third_layer": third_layer, "third_offset": third_offset, "cross_down": cross_down, "cross_up": cross_up, "cross_bias": cross_bias, "cotangent": cotangent}


def silu_slope(value):
    sigmoid = 1.0 / (1.0 + jnp.exp(-value))
    return sigmoid * (1.0 + value * (1.0 - sigmoid))


def bottom_pass(dense_rows, first_layer, first_offset, second_layer, second_offset, third_layer, third_offset):
    first_pre = jnp.dot(dense_rows, first_layer, preferred_element_type=jnp.float32) + first_offset.astype(jnp.float32)
    first_act = jax.nn.silu(first_pre).astype(jnp.bfloat16)
    second_pre = jnp.dot(first_act, second_layer, preferred_element_type=jnp.float32) + second_offset.astype(jnp.float32)
    second_act = jax.nn.silu(second_pre).astype(jnp.bfloat16)
    third_pre = jnp.dot(second_act, third_layer, preferred_element_type=jnp.float32) + third_offset.astype(jnp.float32)
    bottom_out = jax.nn.silu(third_pre).astype(jnp.bfloat16)
    return bottom_out, (first_pre, first_act, second_pre, second_act, third_pre)


def bottom_back(dense_rows, saved, second_layer, third_layer, bottom_grad):
    first_pre, first_act, second_pre, second_act, third_pre = saved
    contract = (((0,), (0,)), ((), ()))
    back_dims = (((1,), (1,)), ((), ()))
    third_delta = (silu_slope(third_pre) * bottom_grad.astype(jnp.float32)).astype(jnp.bfloat16)
    third_grad = lax.dot_general(second_act, third_delta, contract, preferred_element_type=jnp.float32)
    third_bias = jnp.sum(third_delta.astype(jnp.float32), axis=0)
    second_back = lax.dot_general(third_delta, third_layer, back_dims, preferred_element_type=jnp.float32)
    second_delta = (silu_slope(second_pre) * second_back).astype(jnp.bfloat16)
    second_grad = lax.dot_general(first_act, second_delta, contract, preferred_element_type=jnp.float32)
    second_bias = jnp.sum(second_delta.astype(jnp.float32), axis=0)
    first_back = lax.dot_general(second_delta, second_layer, back_dims, preferred_element_type=jnp.float32)
    first_delta = (silu_slope(first_pre) * first_back).astype(jnp.bfloat16)
    first_grad = lax.dot_general(dense_rows, first_delta, contract, preferred_element_type=jnp.float32)
    first_bias = jnp.sum(first_delta.astype(jnp.float32), axis=0)
    parts = (first_grad, first_bias, second_grad, second_bias, third_grad, third_bias)
    return tuple(piece.astype(jnp.float32) for piece in parts)


def zeros_float(shape):
    return jnp.zeros(shape, dtype=jnp.float32)


def reference(dense_feats, lookup_ids, lookup_counts, shard_table, embed_tables, first_layer, first_offset, second_layer, second_offset, third_layer, third_offset, cross_down, cross_up, cross_bias, cotangent):
    group = EX_DEV * N_TABLE
    table_onehot = (shard_table[:, None] == jnp.arange(TABLES, dtype=jnp.int32)[None, :]).astype(jnp.float32)
    slot_iota = jnp.arange(HOT, dtype=jnp.int32)
    back_dims = (((1,), (1,)), ((), ()))

    def pool_one(inputs):
        table_rows, index_rows, count_rows = inputs
        picked = jnp.take(table_rows.astype(jnp.float32), index_rows.astype(jnp.int32), axis=0)
        valid = (count_rows[None, :] > slot_iota[:, None]).astype(jnp.float32)
        return jnp.sum(picked * valid[:, :, None], axis=0).astype(jnp.bfloat16)

    def grad_one(inputs):
        index_rows, count_rows, grad_rows = inputs
        valid = (count_rows[None, :] > slot_iota[:, None]).astype(jnp.float32)
        contrib = valid[:, :, None] * grad_rows.astype(jnp.float32)[None, :, :]
        summed = jax.ops.segment_sum(contrib.reshape(-1, EMB), index_rows.reshape(-1).astype(jnp.int32), num_segments=ROWS)
        return summed.astype(jnp.float32)

    def block_step(running, block_number):
        start = (block_number * group).astype(jnp.int32)
        index_block = lax.dynamic_slice_in_dim(lookup_ids, start, group, 2)
        count_block = lax.dynamic_slice_in_dim(lookup_counts, start, group, 1)
        dense_rows = lax.dynamic_slice_in_dim(dense_feats, start, group, 0)
        cot_rows = lax.dynamic_slice_in_dim(cotangent, start, group, 0)
        pooled = lax.map(pool_one, (embed_tables, index_block, count_block))
        table_pooled = jnp.einsum("sbe,st->bte", pooled.astype(jnp.float32), table_onehot).astype(jnp.bfloat16)
        bottom_out, saved = bottom_pass(dense_rows, first_layer, first_offset, second_layer, second_offset, third_layer, third_offset)
        cross_input = jnp.concatenate([bottom_out[:, None, :], table_pooled], axis=1).reshape(group, CROSS_IN)
        low_rank = jnp.dot(cross_input, cross_down, preferred_element_type=jnp.float32).astype(jnp.bfloat16)
        mixing = jnp.dot(low_rank, cross_up, preferred_element_type=jnp.float32) + cross_bias.astype(jnp.float32)
        cot_float = cot_rows.astype(jnp.float32)
        mix_grad = cot_float * cross_input.astype(jnp.float32)
        bias_part = jnp.sum(mix_grad, axis=0).astype(jnp.float32)
        rank_grad = lax.dot_general(mix_grad.astype(jnp.bfloat16), cross_up, back_dims, preferred_element_type=jnp.float32).astype(jnp.bfloat16)
        input_grad = (cot_float * (mixing + jnp.float32(1.0)) + lax.dot_general(rank_grad, cross_down, back_dims, preferred_element_type=jnp.float32)).astype(jnp.bfloat16)
        input_grad = input_grad.reshape(group, TABLES + 1, EMB)
        bottom_grad = input_grad[:, 0, :]
        shard_grads = jnp.transpose(input_grad[:, 1:, :][:, shard_table, :], (1, 0, 2))
        table_part = lax.map(grad_one, (index_block, count_block, shard_grads)).astype(jnp.float32)
        dense_parts = bottom_back(dense_rows, saved, second_layer, third_layer, bottom_grad)
        table_total, dense_total, bias_total = running
        dense_total = tuple((old + new).astype(jnp.float32) for old, new in zip(dense_total, dense_parts))
        return ((table_total + table_part).astype(jnp.float32), dense_total, (bias_total + bias_part).astype(jnp.float32)), None

    zero_dense = (zeros_float((DENSE, H1)), zeros_float((H1,)), zeros_float((H1, H2)), zeros_float((H2,)), zeros_float((H2, EMB)), zeros_float((EMB,)))
    start_state = (zeros_float((SHARDS, ROWS, EMB)), zero_dense, zeros_float((CROSS_IN,)))
    final_state, unused = lax.scan(block_step, start_state, jnp.arange(N_DP, dtype=jnp.int32))
    table_total, dense_total, bias_total = final_state
    return (table_total, dense_total[0], dense_total[1], dense_total[2], dense_total[3], dense_total[4], dense_total[5], bias_total)
```

```python
import functools

import jax
import jax.numpy as jnp
from jax import lax
from jax.experimental import pallas as pl
from jax.experimental.pallas import tpu as pltpu
from jax.sharding import PartitionSpec as P

TABLES = 26
MESH = pl.DeviceIdType.MESH
BF16 = jnp.bfloat16
F32 = jnp.float32
ROW_TILE = 16
CONTRACT = (((0,), (0,)), ((), ()))
BACK_DIMS = (((1,), (1,)), ((), ()))


def silu_slope(value):
    sigmoid = 1.0 / (1.0 + jnp.exp(-value))
    return sigmoid * (1.0 + value * (1.0 - sigmoid))


def row_code(index):
    low = lax.bitwise_and(index, 127) + 128
    return (low.astype(F32) * lax.shift_left(1, lax.shift_right_logical(index, 7)).astype(F32)).astype(BF16)


def remote(src, dst, send, recv, axis, peer):
    return pltpu.make_async_remote_copy(
        src_ref=src, dst_ref=dst, send_sem=send, recv_sem=recv,
        device_id={axis: peer}, device_id_type=MESH,
    )


def forward_kernel(
    n_table, codes_ref, rowcode_ref, tables_ref, down_ref, up_ref,
    hits_ref, arrived_ref, down_all, up_all,
    hit_buf, table_t, pooled_buf, hit_sem, self_sem, own_sem,
    send_sem, recv_sem, w_send, w_recv, f_send, f_recv,
):
    local_shards, slots, _, batch = codes_ref.shape
    rows = tables_ref.shape[1]
    width = tables_ref.shape[2]
    examples = batch // n_table
    chips = n_table // 2
    lanes = 2 * examples
    me = lax.axis_index("table")
    chip = me // 2
    core = lax.rem(me, 2)
    sibling = chip * 2 + 1 - core

    barrier = pltpu.get_barrier_semaphore()
    for step in range(1, n_table):
        pl.semaphore_signal(
            barrier, inc=1, device_id={"table": lax.rem(me + step, n_table)}, device_id_type=MESH
        )
    own = [
        pltpu.make_async_copy(down_ref, down_all.at[me], own_sem.at[0]),
        pltpu.make_async_copy(up_ref, up_all.at[me], own_sem.at[1]),
    ]
    for copy in own:
        copy.start()
    pl.semaphore_wait(barrier, n_table - 1)

    weights = ((down_ref, down_all), (up_ref, up_all))
    first_stage = []
    for kind, (src, dst) in enumerate(weights):
        for step in range(1, chips):
            peer = lax.rem(chip + step, chips) * 2 + core
            first_stage.append((kind, step, remote(
                src, dst.at[me], w_send.at[kind, step], w_recv.at[kind, step], "table", peer)))
        first_stage.append((kind, 0, remote(
            src, dst.at[me], w_send.at[kind, 0], w_recv.at[kind, 0], "table", sibling)))
    for _, _, copy in first_stage:
        copy.start()

    def send_to(shard, step, other):
        target = lax.rem(chip + step, chips) * 2 + other
        block = pooled_buf.at[shard, step, other]
        return remote(
            block, arrived_ref.at[me, shard], send_sem.at[shard, step, other],
            recv_sem.at[shard, step, core], "table", target)

    def recv_from(shard, step, other):
        source = lax.rem(chip + chips - step, chips) * 2 + other
        return remote(
            pooled_buf.at[shard, step, other], arrived_ref.at[source, shard],
            send_sem.at[shard, step, other], recv_sem.at[shard, step, other], "table", sibling)

    one = jnp.ones((ROW_TILE, lanes), BF16)
    zero = jnp.zeros((ROW_TILE, lanes), BF16)
    for shard in range(local_shards):
        slot = shard % 2
        if shard >= 2:
            pltpu.make_async_copy(hit_buf.at[slot], hits_ref.at[shard - 2], hit_sem.at[shard - 2]).wait()
        table_t[...] = tables_ref[shard].T

        def one_chunk(step):
            target_chip = lax.rem(chip + step, chips)
            start = pl.multiple_of(target_chip * lanes, lanes)
            codes = [codes_ref[shard, h, :, pl.ds(start, lanes)] for h in range(slots)]

            @pl.loop(0, rows // ROW_TILE, unroll=4)
            def _(tile):
                begin = pl.multiple_of(tile * ROW_TILE, ROW_TILE)
                code = rowcode_ref[pl.ds(begin, ROW_TILE), :]
                code = jnp.concatenate([code] * (lanes // 128), axis=1)
                found = [jnp.where(item == code, one, zero) for item in codes]
                while len(found) > 1:
                    found = [found[i] + found[i + 1] for i in range(0, len(found) - 1, 2)] + (
                        [found[-1]] if len(found) % 2 else [])
                hit_buf[slot, pl.ds(begin, ROW_TILE), pl.ds(start, lanes)] = found[0]

            pooled = jnp.dot(
                table_t[...], hit_buf[slot, :, pl.ds(start, lanes)], preferred_element_type=F32)
            pooled = pooled.T.astype(BF16)
            for other in range(2):
                pooled_buf[shard, step, other] = pooled[other * examples:(other + 1) * examples]

        @pl.loop(1, chips)
        def _(step):
            one_chunk(step)
            for other in range(2):
                send_to(shard, step, other).start()

        one_chunk(0)
        send_to(shard, 0, 1 - core).start()
        pltpu.make_async_copy(
            pooled_buf.at[shard, 0, core], arrived_ref.at[me, shard], self_sem.at[shard]).start()
        pltpu.make_async_copy(hit_buf.at[slot], hits_ref.at[shard], hit_sem.at[shard]).start()

    second_stage = []
    for kind, step, copy in first_stage:
        copy.wait_recv()
        if step:
            src = lax.rem(chip + chips - step, chips) * 2 + core
            whole = weights[kind][1]
            forward = remote(
                whole.at[src], whole.at[src], f_send.at[kind, step], f_recv.at[kind, step],
                "table", sibling)
            forward.start()
            second_stage.append(forward)
    for shard in range(local_shards):
        send_to(shard, 0, 1 - core).wait_send()
        recv_from(shard, 0, 1 - core).wait_recv()
        pltpu.make_async_copy(
            pooled_buf.at[shard, 0, core], arrived_ref.at[me, shard], self_sem.at[shard]).wait()
        for step in range(1, chips):
            for other in range(2):
                send_to(shard, step, other).wait_send()
                recv_from(shard, step, other).wait_recv()
    for copy in own:
        copy.wait()
    for _, _, copy in first_stage:
        copy.wait_send()
    for copy in second_stage:
        copy.wait()
    for shard in range(max(0, local_shards - 2), local_shards):
        pltpu.make_async_copy(hit_buf.at[shard % 2], hits_ref.at[shard], hit_sem.at[shard]).wait()


def forward_exchange(n_table, codes, rowcode, tables, down_t, up):
    local_shards, slots, _, batch = codes.shape
    _, rows, width = tables.shape
    examples = batch // n_table
    chips = n_table // 2
    vmem = pl.BlockSpec(memory_space=pltpu.VMEM)
    hbm = pl.BlockSpec(memory_space=pl.ANY)
    dma = pltpu.SemaphoreType.DMA
    return pl.pallas_call(
        functools.partial(forward_kernel, n_table),
        out_shape=(
            jax.ShapeDtypeStruct((local_shards, rows, batch), BF16),
            jax.ShapeDtypeStruct((n_table, local_shards, examples, width), BF16),
            jax.ShapeDtypeStruct((n_table,) + down_t.shape, BF16),
            jax.ShapeDtypeStruct((n_table,) + up.shape, BF16),
        ),
        in_specs=[vmem, vmem, vmem, hbm, hbm],
        out_specs=(hbm, hbm, hbm, hbm),
        scratch_shapes=[
            pltpu.VMEM((2, rows, batch), BF16),
            pltpu.VMEM((width, rows), BF16),
            pltpu.VMEM((local_shards, chips, 2, examples, width), BF16),
            dma((local_shards,)),
            dma((local_shards,)),
            dma((2,)),
            dma((local_shards, chips, 2)),
            dma((local_shards, chips, 2)),
            dma((2, chips)),
            dma((2, chips)),
            dma((2, chips)),
            dma((2, chips)),
        ],
        compiler_params=pltpu.CompilerParams(
            collective_id=0, has_side_effects=True, vmem_limit_bytes=40 * 1024 * 1024),
        name="pool_and_exchange",
    )(codes, rowcode, tables, down_t, up)


def backward_kernel(
    n_table, n_dp, grads_ref, hits_ref, dense_ref, first_pre, first_act, second_pre, second_act,
    third_pre, bottom_grad, second_layer, third_layer, bias_ref,
    table_out, first_out, first_bias, second_out, second_bias, third_out, third_bias, cross_bias,
    hit_buf, got, tab_send, tab_recv, part, edge, part_recv, dp_send, dp_recv, whole,
    hit_sem, a_send, a_recv, t_send, t_recv, p_send, p_recv, d_send, d_recv, w_send, w_recv,
):
    local_shards, rows, batch = hits_ref.shape
    width = grads_ref.shape[3]
    examples = batch // n_table
    chunk = rows // n_dp
    me = lax.axis_index("table")
    level = lax.axis_index("dp")
    share = part_recv.shape[1]

    hit_copies = [
        pltpu.make_async_copy(hits_ref.at[shard], hit_buf.at[shard], hit_sem.at[shard])
        for shard in range(local_shards)
    ]
    for copy in hit_copies:
        copy.start()
    barrier = pltpu.get_barrier_semaphore()
    for step in range(1, n_table):
        pl.semaphore_signal(
            barrier, inc=1, device_id={"table": lax.rem(me + step, n_table)}, device_id_type=MESH)
    for step in range(1, n_dp):
        pl.semaphore_signal(
            barrier, inc=1, device_id={"dp": lax.rem(level + step, n_dp)}, device_id_type=MESH)
    pl.semaphore_wait(barrier, n_table + n_dp - 2)

    def grad_copy(shard, step):
        peer = lax.rem(me + step, n_table)
        return remote(
            grads_ref.at[peer, shard], got.at[shard, me], a_send.at[shard, step],
            a_recv.at[shard, step], "table", peer)

    for shard in range(local_shards):
        for step in range(1, n_table):
            grad_copy(shard, step).start()
        got[shard, me] = grads_ref[me, shard]

    def table_copy(shard, step):
        return remote(
            tab_send.at[shard, step - 1], tab_recv.at[shard, step - 1], t_send.at[shard, step],
            t_recv.at[shard, step], "dp", lax.rem(level + step, n_dp))

    def shard_step(shard):
        for step in range(1, n_table):
            grad_copy(shard, step).wait_recv()
        hit_copies[shard].wait()
        rows_grad = got[shard].reshape(batch, width)

        def product(step):
            begin = pl.multiple_of(lax.rem(level + step, n_dp) * chunk, chunk)
            return jnp.dot(
                hit_buf[shard, pl.ds(begin, chunk), :], rows_grad, preferred_element_type=F32)

        for step in range(1, n_dp):
            tab_send[shard, step - 1] = product(step).astype(BF16)
            table_copy(shard, step).start()
        table_out[shard] = product(0)

    def part_copy(step):
        peer = lax.rem(me + step, n_table)
        return remote(
            part.at[pl.ds(pl.multiple_of(peer * share, 16), share)], part_recv.at[step - 1],
            p_send.at[step], p_recv.at[step], "table", peer)

    def dp_copy(step):
        return remote(
            dp_send, dp_recv.at[step - 1], d_send.at[step], d_recv.at[step], "dp",
            lax.rem(level + step, n_dp))

    def whole_block(index):
        return whole.at[pl.ds(pl.multiple_of(index * share, 16), share)]

    def whole_copy(step):
        return remote(
            whole_block(me), whole_block(me), w_send.at[step], w_recv.at[step], "table",
            lax.rem(me + step, n_table))

    first_width = first_pre.shape[1]
    second_width = second_pre.shape[1]
    pad_in = dense_ref.shape[1]
    first_tiles = first_width // 128
    second_tiles = second_width // 128
    third_base = second_tiles * first_width
    dense_base = third_base + second_width
    edge_base = dense_base + first_tiles * pad_in
    edge_rows = edge.shape[0]

    def bottom_back():
        edge[...] = jnp.zeros_like(edge)
        third_delta = (
            silu_slope(third_pre[...]) * bottom_grad[...].astype(F32)).astype(BF16)
        third_grad = lax.dot_general(
            second_act[...], third_delta, CONTRACT, preferred_element_type=F32)
        part[third_base:third_base + second_width, :] = third_grad.astype(BF16)
        second_back = lax.dot_general(
            third_delta, third_layer[...], BACK_DIMS, preferred_element_type=F32)
        second_delta = (silu_slope(second_pre[...]) * second_back).astype(BF16)
        second_grad = lax.dot_general(
            first_act[...], second_delta, CONTRACT, preferred_element_type=F32).astype(BF16)
        for tile in range(second_tiles):
            part[tile * first_width:(tile + 1) * first_width, :] = second_grad[
                :, tile * 128:(tile + 1) * 128]
        first_back = lax.dot_general(
            second_delta, second_layer[...], BACK_DIMS, preferred_element_type=F32)
        first_delta = (silu_slope(first_pre[...]) * first_back).astype(BF16)
        first_grad = lax.dot_general(
            dense_ref[...], first_delta, CONTRACT, preferred_element_type=F32).astype(BF16)
        for tile in range(first_tiles):
            part[dense_base + tile * pad_in:dense_base + (tile + 1) * pad_in, :] = first_grad[
                :, tile * 128:(tile + 1) * 128]
        row = 0
        for delta, tiles in (
            (first_delta, first_tiles), (second_delta, second_tiles), (third_delta, 1)
        ):
            total = jnp.sum(delta.astype(F32), axis=0, keepdims=True)
            for tile in range(tiles):
                edge[row:row + 1, :] = total[:, tile * 128:(tile + 1) * 128]
                row += 1
        edge[8:8 + bias_ref.shape[0], :] = bias_ref[...]
        part[edge_base:edge_base + edge_rows, :] = edge[...].astype(BF16)
        left = part.shape[0] - edge_base - edge_rows
        if left:
            part[edge_base + edge_rows:, :] = jnp.zeros((left, 128), BF16)

    shard_step(0)
    bottom_back()
    for step in range(1, n_table):
        part_copy(step).start()
    for shard in range(1, local_shards):
        shard_step(shard)

    total = part[pl.ds(pl.multiple_of(me * share, 16), share), :].astype(F32)
    for step in range(1, n_table):
        part_copy(step).wait_recv()
        total = total + part_recv[step - 1].astype(F32)
    dp_send[...] = total.astype(BF16)
    for step in range(1, n_dp):
        dp_copy(step).start()
    for step in range(1, n_dp):
        dp_copy(step).wait_recv()
        total = total + dp_recv[step - 1].astype(F32)
    whole[pl.ds(pl.multiple_of(me * share, 16), share), :] = total.astype(BF16)
    for step in range(1, n_table):
        whole_copy(step).start()

    for shard in range(local_shards):
        for step in range(1, n_dp):
            table_copy(shard, step).wait_recv()
            table_out[shard] += tab_recv[shard, step - 1].astype(F32)
    for step in range(1, n_table):
        whole_copy(step).wait_recv()
    for tile in range(second_tiles):
        second_out[:, tile * 128:(tile + 1) * 128] = whole[
            tile * first_width:(tile + 1) * first_width, :].astype(F32)
    third_out[...] = whole[third_base:third_base + second_width, :].astype(F32)
    for tile in range(first_tiles):
        block = whole[dense_base + tile * pad_in:dense_base + (tile + 1) * pad_in, :].astype(F32)
        first_out[:, tile * 128:(tile + 1) * 128] = block[:first_out.shape[0]]
    edge[...] = whole[edge_base:edge_base + edge_rows, :].astype(F32)
    first_bias[...] = edge[0:first_tiles, :]
    second_bias[...] = edge[first_tiles:first_tiles + second_tiles, :]
    third_bias[...] = edge[first_tiles + second_tiles:first_tiles + second_tiles + 1, :]
    cross_bias[...] = edge[8:8 + cross_bias.shape[0], :]

    for shard in range(local_shards):
        for step in range(1, n_table):
            grad_copy(shard, step).wait_send()
        for step in range(1, n_dp):
            table_copy(shard, step).wait_send()
    for step in range(1, n_table):
        part_copy(step).wait_send()
        whole_copy(step).wait_send()
    for step in range(1, n_dp):
        dp_copy(step).wait_send()


def backward_exchange(n_table, n_dp, grads, hits, dense, first_pre, first_act, second_pre,
                      second_act, third_pre, bottom_grad, second_layer, third_layer, bias_part,
                      dense_width):
    local_shards, rows, batch = hits.shape
    width = grads.shape[3]
    first_width = first_pre.shape[1]
    second_width = second_pre.shape[1]
    bias_rows = bias_part.shape[0]
    edge_rows = -(-(8 + bias_rows) // 16) * 16
    used = (second_width // 128 * first_width + second_width
            + first_width // 128 * dense.shape[1] + edge_rows)
    share = -(-used // (16 * n_table)) * 16
    vmem = pl.BlockSpec(memory_space=pltpu.VMEM)
    hbm = pl.BlockSpec(memory_space=pl.ANY)
    dma = pltpu.SemaphoreType.DMA
    shapes = (
        (local_shards, rows // n_dp, width), (dense_width, first_width), (first_width // 128, 128),
        (first_width, second_width), (second_width // 128, 128), (second_width, width), (1, 128),
        (bias_rows, 128),
    )
    return pl.pallas_call(
        functools.partial(backward_kernel, n_table, n_dp),
        out_shape=tuple(jax.ShapeDtypeStruct(shape, F32) for shape in shapes),
        in_specs=[vmem, hbm] + [vmem] * 10,
        out_specs=(vmem,) * 8,
        scratch_shapes=[
            pltpu.VMEM((local_shards, rows, batch), BF16),
            pltpu.VMEM((local_shards, n_table, batch // n_table, width), BF16),
            pltpu.VMEM((local_shards, n_dp - 1, rows // n_dp, width), BF16),
            pltpu.VMEM((local_shards, n_dp - 1, rows // n_dp, width), BF16),
            pltpu.VMEM((n_table * share, 128), BF16),
            pltpu.VMEM((edge_rows, 128), F32),
            pltpu.VMEM((n_table - 1, share, 128), BF16),
            pltpu.VMEM((share, 128), BF16),
            pltpu.VMEM((n_dp - 1, share, 128), BF16),
            pltpu.VMEM((n_table * share, 128), BF16),
            dma((local_shards,)),
            dma((local_shards, n_table)),
            dma((local_shards, n_table)),
            dma((local_shards, n_dp)),
            dma((local_shards, n_dp)),
            dma((n_table,)),
            dma((n_table,)),
            dma((n_dp,)),
            dma((n_dp,)),
            dma((n_table,)),
            dma((n_table,)),
        ],
        compiler_params=pltpu.CompilerParams(
            collective_id=1, has_side_effects=True, vmem_limit_bytes=48 * 1024 * 1024),
        name="gradient_exchange",
    )(grads, hits, dense, first_pre, first_act, second_pre, second_act, third_pre, bottom_grad,
      second_layer, third_layer, bias_part)


def bottom_pass(
    dense_rows, first_layer, first_offset, second_layer, second_offset, third_layer, third_offset
):
    first_pre = jnp.dot(dense_rows, first_layer, preferred_element_type=F32) + first_offset
    first_act = jax.nn.silu(first_pre).astype(BF16)
    second_pre = jnp.dot(first_act, second_layer, preferred_element_type=F32) + second_offset
    second_act = jax.nn.silu(second_pre).astype(BF16)
    third_pre = jnp.dot(second_act, third_layer, preferred_element_type=F32) + third_offset
    bottom_out = jax.nn.silu(third_pre).astype(BF16)
    return (bottom_out, (first_pre, first_act, second_pre, second_act, third_pre))


def local(
    n_table,
    n_dp,
    dense_feats,
    lookup_ids,
    lookup_counts,
    shard_table,
    embed_tables,
    first_layer,
    first_offset,
    second_layer,
    second_offset,
    third_layer,
    third_offset,
    cross_down,
    cross_up,
    cross_bias,
    cotangent,
):
    local_shards, rows, width = embed_tables.shape
    slots, batch = lookup_ids.shape[1:]
    examples, dense_width = dense_feats.shape
    shard_total = local_shards * n_table

    slot_iota = lax.broadcasted_iota(jnp.int32, (1, slots, 1), 1)
    codes = jnp.where(lookup_counts[:, None, :] > slot_iota, row_code(lookup_ids), 0).astype(BF16)
    codes = jnp.broadcast_to(codes[:, :, None, :], (local_shards, slots, ROW_TILE, batch))
    rowcode = row_code(lax.broadcasted_iota(jnp.int32, (rows, 128), 0))
    hits, arrived, down_all, up_all = forward_exchange(
        n_table, codes, rowcode, embed_tables, cross_down.T, cross_up)
    down_t = down_all.reshape(-1, cross_up.shape[1])
    up_whole = up_all.reshape(-1, cross_up.shape[1])

    table_onehot = (
        shard_table[:, None] == lax.broadcasted_iota(jnp.int32, (shard_total, TABLES), 1)
    ).astype(BF16)
    table_pooled = jnp.einsum(
        "sbe,st->bte", arrived.reshape(shard_total, examples, width), table_onehot,
        preferred_element_type=F32).astype(BF16)
    bottom_out, saved = bottom_pass(
        dense_feats, first_layer, first_offset, second_layer, second_offset, third_layer,
        third_offset)
    cross_input = jnp.concatenate([bottom_out[:, None, :], table_pooled], axis=1).reshape(
        examples, -1)
    low_rank = lax.dot_general(
        cross_input, down_t, BACK_DIMS, preferred_element_type=F32).astype(BF16)
    mixing = jnp.dot(low_rank, up_whole, preferred_element_type=F32) + cross_bias
    cot_float = cotangent.astype(F32)
    mix_grad = cot_float * cross_input.astype(F32)
    bias_part = jnp.sum(mix_grad, axis=0)
    rank_grad = lax.dot_general(
        mix_grad.astype(BF16), up_whole, BACK_DIMS, preferred_element_type=F32).astype(BF16)
    input_grad = (
        cot_float * (mixing + 1.0) + jnp.dot(rank_grad, down_t, preferred_element_type=F32)
    ).astype(BF16)
    bottom_grad = input_grad[:, :width]
    shard_grads = jnp.einsum(
        "bte,st->sbe", input_grad.reshape(examples, TABLES + 1, width)[:, 1:, :], table_onehot,
        preferred_element_type=F32).astype(BF16)
    dense_pad = jnp.pad(dense_feats, ((0, 0), (0, -dense_width % 16)))
    outs = backward_exchange(
        n_table, n_dp, shard_grads.reshape(n_table, local_shards, examples, width), hits,
        dense_pad, *saved, bottom_grad, second_layer, third_layer, bias_part.reshape(-1, 128),
        dense_width)
    return (outs[0], outs[1], outs[2].reshape(-1), outs[3], outs[4].reshape(-1), outs[5],
            outs[6].reshape(-1), outs[7].reshape(-1))


def solution(mesh):
    placed = (
        P(("dp", "table"), None),
        P("table", None, "dp"),
        P("table", "dp"),
        P(),
        P("table", None, None),
        P(),
        P(),
        P(),
        P(),
        P(),
        P(),
        P(None, "table"),
        P("table", None),
        P(),
        P(("dp", "table"), None),
    )
    return jax.shard_map(
        functools.partial(local, mesh.shape["table"], mesh.shape["dp"]),
        mesh=mesh,
        in_specs=placed,
        out_specs=(P("table", "dp", None), P(), P(), P(), P(), P(), P(), P()),
        check_vma=False,
    )
```
